32 devices in a mesh: ctx: 8 (over y, x, core), rep: 4 (over z).
Axes of the slice: x: 2, y: 2, z: 4, core: 2. Of those that a mesh axis runs over, the one named last changes fastest.
Arguments:
- inputs: bfloat16 [4, 2048, 256], P('rep', 'ctx'), may hold values from -6 to 6
- w_expand: bfloat16 [512, 1024], replicated, may hold values from -0.25 to 0.25
- b_expand: float32 [1024], replicated, may hold values from -1 to 1
- w_reduce: bfloat16 [1024, 512], replicated, may hold values from -0.1875 to 0.1875
- b_reduce: float32 [512], replicated, may hold values from -0.5 to 0.5
- gate_logit: float32 [512], replicated, may hold values from -2 to 2
- cotangent: bfloat16 [4, 2048, 256], P('rep', 'ctx'), may hold values from -6 to 6
Outputs:
- outputs: bfloat16 [4, 2048, 256], P('rep', 'ctx')
- grad_inputs: bfloat16 [4, 2048, 256], P('rep', 'ctx')
- grad_w_expand: float32 [512, 1024], P('ctx')
- grad_b_expand: float32 [1024], replicated
- grad_w_reduce: float32 [1024, 512], P('ctx')
- grad_b_reduce: float32 [512], replicated
- grad_gate: float32 [512], replicated
The draws below stay inside these ranges and needn't reach their ends.
All inputs are finite; a program needn't handle non-finite values.
Results may differ from the reference program's by a relative error of at most 0.018.
Values may be sent and summed in bfloat16 or wider, within the bound.
No kernel may reach another device: no remote copies, remote signals or barrier semaphores. Data moves between devices by JAX's collectives and lax.ppermute only.
A program may use at most 64 MiB of HBM per device.

```python
import math
import jax
import jax.numpy as jnp
from jax import lax

M = 256
H = 1024
P_DEV = 256
SECTIONS = 4
SEQS = 4
LENGTH = 2048
N_CTX = 8


def level_of(key, dims, cuts, least, high):
    def one(dim, blocks):
        steps = jax.random.uniform(jax.random.fold_in(jax.random.fold_in(key, 6), dim), (blocks,), jnp.float32, least / len(cuts), high / len(cuts))
        return jnp.repeat(jnp.exp(steps), dims[dim] // blocks).reshape((-1,) + (1,) * (len(dims) - dim - 1))

    level = one(*cuts[0])
    for cut in cuts[1:]:
        level = level * one(*cut)
    return level


def gaussian(rng, dims, deviation, reach, split=(), kind=jnp.bfloat16):
    entries = deviation * jax.random.normal(rng, dims, jnp.float32)
    if split:
        entries = entries * level_of(rng, dims, split, -0.22, 0.18)
    return jnp.clip(entries, -reach, reach).astype(kind)


def setup_inputs(seed: int = 0) -> dict:
    splits = jax.random.split(jax.random.key(seed), 8)
    inputs = gaussian(splits[0], (SEQS, LENGTH, M), 1.0, 6.0, ((0, 4), (1, 8)))
    w_expand = gaussian(splits[1], (2 * M, H), (2 * M) ** -0.5, 0.25)
    b_expand = jnp.clip(jax.random.uniform(splits[2], (H,), jnp.float32, -1.0, 1.0), -1.0, 1.0)
    w_reduce = gaussian(splits[3], (H, 2 * M), H ** -0.5, 0.1875)
    b_reduce = jnp.clip(jax.random.uniform(splits[4], (2 * M,), jnp.float32, -0.5, 0.5), -0.5, 0.5)
    gate_logit = jnp.clip(jax.random.uniform(splits[5], (2 * M,), jnp.float32, -2.0, 2.0), -2.0, 2.0)
    cotangent = gaussian(splits[6], (SEQS, LENGTH, M), 1.0, 6.0, ((0, 4), (1, 8)))
    return dict(inputs=inputs, w_expand=w_expand, b_expand=b_expand, w_reduce=w_reduce, b_reduce=b_reduce, gate_logit=gate_logit, cotangent=cotangent)


EPSILON = 1e-05

def gelu_back(preact, upstream):
    return jax.vjp(lambda value: jax.nn.gelu(value, approximate=False), preact)[1](upstream)[0]

def switch_forward(lower, upper, w_expand, b_expand):
    joined = jnp.concatenate([lower, upper], axis=-1).astype(jnp.float32)
    centred = joined - lax.optimization_barrier(jnp.mean(joined, axis=-1, keepdims=True))
    inv_std = lax.rsqrt(lax.optimization_barrier(jnp.mean(centred * centred, axis=-1, keepdims=True)) + EPSILON)
    normed = centred * inv_std
    normed_low = normed.astype(jnp.bfloat16)
    preact = jnp.dot(normed_low, w_expand, preferred_element_type=jnp.float32) + b_expand
    hidden = jax.nn.gelu(preact, approximate=False).astype(jnp.bfloat16)
    return (joined, normed, inv_std, normed_low, preact, hidden)

def switch_apply(lower, upper, w_expand, b_expand, w_reduce, b_reduce, gate_logit):
    joined, normed, inv_std, normed_low, preact, hidden = switch_forward(lower, upper, w_expand, b_expand)
    mixed = jnp.dot(hidden, w_reduce, preferred_element_type=jnp.float32)
    result = (jax.nn.sigmoid(gate_logit) * joined + mixed + b_reduce).astype(jnp.bfloat16)
    width = lower.shape[-1]
    return (result[:, :width], result[:, width:])

def switch_backward(lower, upper, grad_lower, grad_upper, w_expand, b_expand, w_reduce, b_reduce, gate_logit):
    joined, normed, inv_std, normed_low, preact, hidden = switch_forward(lower, upper, w_expand, b_expand)
    grad_out = jnp.concatenate([grad_lower, grad_upper], axis=-1)
    grad_float = grad_out.astype(jnp.float32)
    sigma = jax.nn.sigmoid(gate_logit)
    grad_bias_red = lax.optimization_barrier(jnp.sum(grad_float, axis=0))
    grad_gate = lax.optimization_barrier(jnp.sum(grad_float * joined, axis=0)) * sigma * (1.0 - sigma)
    grad_weight_red = jnp.dot(hidden.T, grad_out, preferred_element_type=jnp.float32)
    grad_hidden = jnp.dot(grad_out, w_reduce.T, preferred_element_type=jnp.float32)
    grad_pre = gelu_back(preact, grad_hidden)
    grad_pre_low = grad_pre.astype(jnp.bfloat16)
    grad_bias_exp = lax.optimization_barrier(jnp.sum(grad_pre, axis=0))
    grad_weight_exp = jnp.dot(normed_low.T, grad_pre_low, preferred_element_type=jnp.float32)
    grad_normed = jnp.dot(grad_pre_low, w_expand.T, preferred_element_type=jnp.float32)
    grad_joined = sigma * grad_float + inv_std * (grad_normed - lax.optimization_barrier(jnp.mean(grad_normed, axis=-1, keepdims=True)) - normed * lax.optimization_barrier(jnp.mean(grad_normed * normed, axis=-1, keepdims=True)))
    grad_joined = grad_joined.astype(jnp.bfloat16)
    width = lower.shape[-1]
    return (grad_joined[:, :width], grad_joined[:, width:], (grad_weight_exp, grad_bias_exp, grad_weight_red, grad_bias_red, grad_gate))

def split_pairs(state, block):
    seqs, length, width = state.shape
    groups = length // (2 * block)
    view = state.reshape(seqs, groups, 2, block, width)
    return (view[:, :, 0].reshape(-1, width), view[:, :, 1].reshape(-1, width))

def join_pairs(first, second, shape, block):
    seqs, length, width = shape
    groups = length // (2 * block)
    return jnp.stack([first.reshape(seqs, groups, block, width), second.reshape(seqs, groups, block, width)], axis=2).reshape(seqs, length, width)

def reference(inputs, w_expand, b_expand, w_reduce, b_reduce, gate_logit, cotangent):
    weights = (w_expand, b_expand, w_reduce, b_reduce, gate_logit)
    count = N_CTX.bit_length() - 1
    bits = [(count - 1 - section) % count for section in range(SECTIONS)]
    shape = inputs.shape
    state = inputs
    saved = []
    for bit in bits:
        block = P_DEV * 2 ** bit
        lower, upper = split_pairs(state, block)
        saved.append((lower, upper))
        out_lower, out_upper = switch_apply(lower, upper, *weights)
        state = join_pairs(out_lower, out_upper, shape, block)
    outputs = state
    grad_state = cotangent
    totals = (jnp.zeros(w_expand.shape, jnp.float32), jnp.zeros(b_expand.shape, jnp.float32), jnp.zeros(w_reduce.shape, jnp.float32), jnp.zeros(b_reduce.shape, jnp.float32), jnp.zeros(gate_logit.shape, jnp.float32))
    for section in reversed(range(SECTIONS)):
        block = P_DEV * 2 ** bits[section]
        lower, upper = saved[section]
        grad_lower, grad_upper = split_pairs(grad_state, block)
        back_lower, back_upper, grads = switch_backward(lower, upper, grad_lower, grad_upper, *weights)
        totals = tuple((total + piece for total, piece in zip(totals, grads)))
        grad_state = join_pairs(back_lower, back_upper, shape, block)
    factor = 1.0 / math.sqrt(shape[0] * shape[1])
    return (outputs, grad_state, totals[0] * factor, totals[1] * factor, totals[2] * factor, totals[3] * factor, totals[4] * factor)
```

```python
import functools
import math

import jax
import jax.numpy as jnp
from jax import lax
from jax.experimental import pallas as pl
from jax.experimental.pallas import tpu as pltpu
from jax.sharding import PartitionSpec as P

SECTIONS = 4
EPSILON = 1e-05
EXTRA = 16
F32 = jnp.float32
BF16 = jnp.bfloat16

ROOT = 0.3275911
COEFFS = (0.254829592, -0.284496736, 1.421413741, -1.453152027, 1.061405429)


def gelu_pair(x):
    bell = jnp.exp(-0.5 * x * x)
    t = 1.0 / (1.0 + (ROOT * math.sqrt(0.5)) * jnp.abs(x))
    poly = COEFFS[4]
    for a in (COEFFS[3], COEFFS[2], COEFFS[1], COEFFS[0]):
        poly = poly * t + a
    tail = (0.5 * poly * t) * bell
    cdf = jnp.where(x < 0.0, tail, 1.0 - tail)
    return x * cdf, cdf + x * bell * (1.0 / math.sqrt(2.0 * math.pi))


def split_parts(x):
    high = x.astype(BF16).astype(F32)
    return high, x - high


def write_extra(refs, small):
    high, low = split_parts(small)
    pad = jnp.zeros((EXTRA // 2 - small.shape[0], small.shape[1]), F32)
    rows = jnp.concatenate([high, pad, low, pad], axis=0).astype(BF16)
    for ref in refs:
        ref[ref.shape[0] - EXTRA :, :] = rows


def read_extra(ref, count):
    rows = ref[ref.shape[0] - EXTRA :, :].astype(F32)
    return rows[:count] + rows[EXTRA // 2 : EXTRA // 2 + count]


def slabs_of(order, ctx_bits, me_ctx, me_rep):
    count = 2 ** len(order)
    slabs = []
    for q in range(count):
        flip_ctx, flip_rep = 0, 0
        for place, (axis, bit) in enumerate(order):
            if q >> (len(order) - 1 - place) & 1:
                if axis == "ctx":
                    flip_ctx |= bit
                else:
                    flip_rep |= bit
        slabs.append((me_ctx ^ flip_ctx, (me_rep & 1) ^ flip_rep))
    return slabs


def main_kernel(
    blocks, order_a, order_b, where_ref, moved_ref, we_ref, be_ref, wr_ref, br_ref, gate_ref,
    back_ref, send_a, keep_a, send_b, keep_b,
    normed_s, low_s, hid_s, slope_s, gpre_s, gout_s, rstd_s, joined_s, acc_e, acc_r,
):
    groups, _, rows, width = moved_ref.shape
    pairs = groups * rows // 2
    both = 2 * width
    sigma = jax.nn.sigmoid(gate_ref[...])

    def gather(get, block):
        low = [g for g in range(groups) if not g & block]
        first = jnp.concatenate([get(g) for g in low], axis=0)
        second = jnp.concatenate([get(g | block) for g in low], axis=0)
        return jnp.concatenate([first, second], axis=1)

    def scatter(put, value, block):
        low = [g for g in range(groups) if not g & block]
        for i, g in enumerate(low):
            piece = value[i * rows : (i + 1) * rows]
            put(g, piece[:, :width])
            put(g | block, piece[:, width:])

    for s, block in enumerate(blocks):
        source = moved_ref if s == 0 else back_ref
        joined = gather(lambda g: source[g, 0], block).astype(F32)
        centred = joined - jnp.mean(joined, axis=-1, keepdims=True)
        rstd = lax.rsqrt(jnp.mean(centred * centred, axis=-1, keepdims=True) + EPSILON)
        normed = centred * rstd
        low = normed.astype(BF16)
        here = pl.ds(s * pairs, pairs)
        normed_s[here, :] = normed
        joined_s[here, :] = joined
        low_s[here, :] = low
        rstd_s[here, :] = rstd
        preact = jnp.dot(low, we_ref[...], preferred_element_type=F32) + be_ref[...]
        hidden, slope = gelu_pair(preact)
        hidden = hidden.astype(BF16)
        hid_s[here, :] = hidden
        slope_s[here, :] = slope
        mixed = jnp.dot(hidden, wr_ref[...], preferred_element_type=F32)
        result = (sigma * joined + mixed + br_ref[...]).astype(BF16)

        def put(g, piece):
            back_ref[g, 0] = piece

        scatter(put, result, block)

    sum_be = jnp.zeros((1, we_ref.shape[1]), F32)
    sum_br = jnp.zeros((1, both), F32)
    sum_gate = jnp.zeros((1, both), F32)
    for s in reversed(range(len(blocks))):
        block = blocks[s]
        here = pl.ds(s * pairs, pairs)
        source = moved_ref if s == len(blocks) - 1 else back_ref
        gout = gather(lambda g: source[g, 1], block)
        gout_s[here, :] = gout
        gfloat = gout.astype(F32)
        sum_br += jnp.sum(gfloat, axis=0, keepdims=True)
        sum_gate += jnp.sum(gfloat * joined_s[here, :], axis=0, keepdims=True)
        ghidden = lax.dot_general(gout, wr_ref[...], (((1,), (1,)), ((), ())), preferred_element_type=F32)
        gpre = ghidden * slope_s[here, :]
        sum_be += jnp.sum(gpre, axis=0, keepdims=True)
        gpre = gpre.astype(BF16)
        gpre_s[here, :] = gpre
        gnormed = lax.dot_general(gpre, we_ref[...], (((1,), (1,)), ((), ())), preferred_element_type=F32)
        normed = normed_s[here, :]
        inner = gnormed - jnp.mean(gnormed, axis=-1, keepdims=True)
        inner = inner - normed * jnp.mean(gnormed * normed, axis=-1, keepdims=True)
        gjoined = (sigma * gfloat + rstd_s[here, :] * inner).astype(BF16)

        def put(g, piece):
            back_ref[g, 1] = piece

        scatter(put, gjoined, block)

    rows_t = (((0,), (0,)), ((), ()))
    acc_e[...] = lax.dot_general(low_s[...], gpre_s[...], rows_t, preferred_element_type=F32)
    acc_r[...] = lax.dot_general(hid_s[...], gout_s[...], rows_t, preferred_element_type=F32)

    me_ctx, me_rep = where_ref[0], where_ref[1]
    slabs = slabs_of(order_a, None, me_ctx, me_rep)
    half = len(slabs) // 2
    size = acc_e.shape[0] * acc_e.shape[1] // (both * len(slabs))
    for q, (shard, side) in enumerate(slabs):
        target, at = (keep_a, q) if q < half else (send_a, q - half)
        row = pl.multiple_of(shard * size, size)
        lane = pl.multiple_of(side * both, both)
        target[at * size : (at + 1) * size, :] = acc_e[pl.ds(row, size), pl.ds(lane, both)].astype(BF16)
    slabs = slabs_of(order_b, None, me_ctx, me_rep)
    for q, (shard, side) in enumerate(slabs):
        target, at = (keep_b, q) if q < half else (send_b, q - half)
        row = pl.multiple_of((shard * 2 + side) * size, size)
        target[at * size : (at + 1) * size, :] = acc_r[pl.ds(row, size), :].astype(BF16)
    small = jnp.concatenate(
        [sum_be[:, :both], sum_be[:, both:], sum_br, sum_gate * sigma * (1.0 - sigma)], axis=0
    )
    write_extra((send_a, keep_a), small)


def halve_kernel(extra, keep_ref, recv_ref, send_out, keep_out):
    half = (keep_ref.shape[0] - extra) // 2
    for out, start in ((keep_out, 0), (send_out, half)):
        span = slice(start, start + half)
        out[:half, :] = (keep_ref[span, :].astype(F32) + recv_ref[span, :].astype(F32)).astype(BF16)
    if extra:
        write_extra((send_out, keep_out), read_extra(keep_ref, 4) + read_extra(recv_ref, 4))


def add_kernel(extra, keep_ref, recv_ref, out_ref):
    size = keep_ref.shape[0] - extra
    out_ref[:size, :] = (keep_ref[:size, :].astype(F32) + recv_ref[:size, :].astype(F32)).astype(BF16)
    if extra:
        write_extra((out_ref,), read_extra(keep_ref, 4) + read_extra(recv_ref, 4))


def final_kernel(factor, where_ref, own_a, other_a, own_b, other_b, out_e, out_be, out_r, out_br, out_gate):
    side = where_ref[1] & 1
    size, lanes = own_b.shape
    rows = pl.multiple_of(side * size, size)
    rest = pl.multiple_of((1 - side) * size, size)
    out_r[pl.ds(rows, size), :] = own_b[...].astype(F32) * factor
    out_r[pl.ds(rest, size), :] = other_b[...].astype(F32) * factor
    here = pl.multiple_of(side * lanes, lanes)
    there = pl.multiple_of((1 - side) * lanes, lanes)
    out_e[:, pl.ds(here, lanes)] = own_a[:size, :].astype(F32) * factor
    out_e[:, pl.ds(there, lanes)] = other_a[...].astype(F32) * factor
    small = read_extra(own_a, 4) * factor
    out_be[:, :lanes] = small[0:1]
    out_be[:, lanes:] = small[1:2]
    out_br[...] = small[2:3]
    out_gate[...] = small[3:4]


VMEM = pl.BlockSpec(memory_space=pltpu.VMEM)
SMEM = pl.BlockSpec(memory_space=pltpu.SMEM)


def call(kernel, name, shapes, args, scratch=(), scalars=0):
    return pl.pallas_call(
        kernel,
        name=name,
        out_shape=shapes,
        in_specs=[SMEM] * scalars + [VMEM] * (len(args) - scalars),
        out_specs=[VMEM] * len(shapes),
        scratch_shapes=scratch,
        compiler_params=pltpu.CompilerParams(vmem_limit_bytes=48 * 2**20),
    )(*args)


def rows_of(count, lanes):
    return jax.ShapeDtypeStruct((count, lanes), BF16)


def swap(value, axis, bit):
    return lax.ppermute(value, axis, [(i, i ^ bit) for i in range(lax.axis_size(axis))])


def body(inputs, w_expand, b_expand, w_reduce, b_reduce, gate_logit, cotangent):
    rows, width = inputs.shape[1:]
    devs, reps = lax.axis_size("ctx"), lax.axis_size("rep")
    slice_rows = rows // devs
    count = devs.bit_length() - 1
    groups = min(devs, 2**SECTIONS)
    inner = devs // groups
    blocks = [2 ** ((count - 1 - s) % count) // inner for s in range(SECTIONS)]
    both, hid = w_expand.shape

    ctx_bits = [("ctx", 2**i) for i in range(count)]
    rep_bits = [("rep", 2**i) for i in range(reps.bit_length() - 1)]
    order_a = ctx_bits + rep_bits[:1]
    order_b = ctx_bits[:1] + ctx_bits[2:] + rep_bits[:1] + ctx_bits[1:2]
    where = jnp.stack([lax.axis_index("ctx"), lax.axis_index("rep")]).astype(jnp.int32)

    packed = jnp.stack([inputs.reshape(devs, slice_rows, width), cotangent.reshape(devs, slice_rows, width)], axis=1)
    moved = lax.all_to_all(packed, "ctx", split_axis=0, concat_axis=0, tiled=True)
    moved = moved.reshape(groups, inner, 2, slice_rows, width).swapaxes(1, 2)
    moved = moved.reshape(groups, 2, inner * slice_rows, width)

    pairs = rows // 2
    total = SECTIONS * pairs
    half = both * hid // both // 2
    back, send_a, keep_a, send_b, keep_b = call(
        functools.partial(main_kernel, blocks, order_a, order_b),
        "sections",
        [
            jax.ShapeDtypeStruct(moved.shape, BF16),
            rows_of(half + EXTRA, both),
            rows_of(half + EXTRA, both),
            rows_of(half, both),
            rows_of(half, both),
        ],
        (where, moved, w_expand, b_expand[None], w_reduce, b_reduce[None], gate_logit[None]),
        [
            pltpu.VMEM((total, both), F32),
            pltpu.VMEM((total, both), BF16),
            pltpu.VMEM((total, hid), BF16),
            pltpu.VMEM((total, hid), F32),
            pltpu.VMEM((total, hid), BF16),
            pltpu.VMEM((total, both), BF16),
            pltpu.VMEM((total, 1), F32),
            pltpu.VMEM((total, both), F32),
            pltpu.VMEM((both, hid), F32),
            pltpu.VMEM((hid, both), F32),
        ],
        scalars=1,
    )

    back = back.reshape(groups, 2, inner, slice_rows, width).swapaxes(1, 2).reshape(devs, 2, slice_rows, width)
    home = lax.all_to_all(back, "ctx", split_axis=0, concat_axis=0, tiled=True)
    outputs = home[:, 0].reshape(inputs.shape)
    grad_inputs = home[:, 1].reshape(inputs.shape)

    def halve(send, keep, order, extra):
        for step, (axis, bit) in enumerate(order):
            received = swap(send, axis, bit)
            if step + 1 == len(order):
                return call(functools.partial(add_kernel, extra), "add", [rows_of(*keep.shape)], (keep, received))[0]
            size = (keep.shape[0] - extra) // 2 + extra
            send, keep = call(
                functools.partial(halve_kernel, extra), "halve", [rows_of(size, both)] * 2, (keep, received)
            )

    own_a = halve(send_a, keep_a, order_a, EXTRA)
    own_b = halve(send_b, keep_b, order_b, 0)
    for axis, bit in rep_bits[1:]:
        got_a, got_b = swap(own_a, axis, bit), swap(own_b, axis, bit)
        own_a = call(functools.partial(add_kernel, EXTRA), "add", [rows_of(*own_a.shape)], (own_a, got_a))[0]
        own_b = call(functools.partial(add_kernel, 0), "add", [rows_of(*own_b.shape)], (own_b, got_b))[0]
    size = own_b.shape[0]
    other_a, other_b = swap(own_a[:size], "rep", 1), swap(own_b, "rep", 1)
    factor = 1.0 / math.sqrt(reps * devs * rows)
    grad_e, grad_be, grad_r, grad_br, grad_gate = call(
        functools.partial(final_kernel, factor),
        "final",
        [
            jax.ShapeDtypeStruct((both // devs, hid), F32),
            jax.ShapeDtypeStruct((1, hid), F32),
            jax.ShapeDtypeStruct((hid // devs, both), F32),
            jax.ShapeDtypeStruct((1, both), F32),
            jax.ShapeDtypeStruct((1, both), F32),
        ],
        (where, own_a, other_a, own_b, other_b),
        scalars=1,
    )
    return outputs, grad_inputs, grad_e, grad_be[0], grad_r, grad_br[0], grad_gate[0]


def solution(mesh):
    return jax.shard_map(
        body,
        mesh=mesh,
        in_specs=(P("rep", "ctx", None), P(), P(), P(), P(), P(), P("rep", "ctx", None)),
        out_specs=(
            P("rep", "ctx", None),
            P("rep", "ctx", None),
            P("ctx", None),
            P(),
            P("ctx", None),
            P(),
            P(),
        ),
        check_vma=False,
    )
```

```python
import functools
import math

import jax
import jax.numpy as jnp
from jax import lax
from jax.experimental import pallas as pl
from jax.experimental.pallas import tpu as pltpu
from jax.sharding import PartitionSpec as P

SECTIONS = 4
EPSILON = 1e-05
EXTRA = 16
F32 = jnp.float32
BF16 = jnp.bfloat16

ROOT = 0.3275911
COEFFS = (0.254829592, -0.284496736, 1.421413741, -1.453152027, 1.061405429)


def gelu_pair(x):
    bell = jnp.exp(-0.5 * x * x)
    t = 1.0 / (1.0 + (ROOT * math.sqrt(0.5)) * jnp.abs(x))
    poly = COEFFS[4]
    for a in (COEFFS[3], COEFFS[2], COEFFS[1], COEFFS[0]):
        poly = poly * t + a
    tail = (0.5 * poly * t) * bell
    cdf = jnp.where(x < 0.0, tail, 1.0 - tail)
    return x * cdf, cdf + x * bell * (1.0 / math.sqrt(2.0 * math.pi))


def split_parts(x):
    high = x.astype(BF16).astype(F32)
    return high, x - high


def write_extra(refs, small):
    high, low = split_parts(small)
    pad = jnp.zeros((EXTRA // 2 - small.shape[0], small.shape[1]), F32)
    rows = jnp.concatenate([high, pad, low, pad], axis=0).astype(BF16)
    for ref in refs:
        ref[ref.shape[0] - EXTRA :, :] = rows


def read_extra(ref, count):
    rows = ref[ref.shape[0] - EXTRA :, :].astype(F32)
    return rows[:count] + rows[EXTRA // 2 : EXTRA // 2 + count]


def slabs_of(order, me_ctx, me_rep):
    count = 2 ** len(order)
    slabs = []
    for q in range(count):
        flip_ctx, flip_rep = 0, 0
        for place, (axis, bit) in enumerate(order):
            if q >> (len(order) - 1 - place) & 1:
                if axis == "ctx":
                    flip_ctx |= bit
                else:
                    flip_rep |= bit
        slabs.append((me_ctx ^ flip_ctx, (me_rep & 1) ^ flip_rep))
    return slabs


def prep_kernel(we_ref, be_ref, wr_ref, br_ref, gate_ref, we_out, wet_out, wr_out, wrt_out, be_out, br_out, gate_out, sems):
    pairs = (
        (we_ref, we_out), (wr_ref, wr_out), (be_ref, be_out), (br_ref, br_out), (gate_ref, gate_out),
    )
    copies = [pltpu.make_async_copy(a, b, sems.at[i]) for i, (a, b) in enumerate(pairs)]
    for copy in copies:
        copy.start()
    copies[0].wait()
    wet_out[...] = we_out[...].T
    copies[1].wait()
    wrt_out[...] = wr_out[...].T
    for copy in copies[2:]:
        copy.wait()


def pack_kernel(where_ref, inputs_ref, cot_ref, send_ref, keep_ref, inputs_s, cot_s, sems):
    me = where_ref[0]
    chips, _, rows, _ = send_ref.shape
    sources = (inputs_s, cot_s)
    copies = [pltpu.make_async_copy(a, b, sems.at[i]) for i, (a, b) in enumerate(zip((inputs_ref, cot_ref), sources))]
    for copy in copies:
        copy.start()
    for which, source in enumerate(sources):
        copies[which].wait()
        for k in range(chips):
            for out, to in ((send_ref, me ^ (2 * k) ^ 1), (keep_ref, me ^ (2 * k))):
                out[k, which] = source[pl.ds(pl.multiple_of(to * rows, rows), rows), :]


def relay_kernel(keep_ref, got_ref, *outs):
    for k, out in enumerate(outs, 1):
        out[0] = keep_ref[k]
        out[1] = got_ref[k]


def main_kernel(blocks, chains, pieces, where_ref, *refs):
    arrived, refs = refs[:pieces], refs[pieces:]
    (
        we_ref, wet_ref, wr_ref, wrt_ref, be_ref, br_ref, gate_ref,
    ) = refs[:7]
    back_ref, messages, refs = refs[7], refs[8 : 8 + 2 * len(chains)], refs[8 + 2 * len(chains) :]
    (
        normed_s, low_s, hid_s, slope_s, gpre_s, gout_s, rstd_s, joined_s, acc_e, acc_r, *moved_s,
    ) = refs
    if pieces == 1:
        moved_ref = arrived[0]
    else:
        moved_ref = moved_s[0]
        keep_ref, got_ref, *relayed = arrived
        for core, ref in enumerate((keep_ref, got_ref)):
            moved_ref[where_ref[0] ^ core] = ref[0]
        for k, ref in enumerate(relayed, 1):
            for core in range(2):
                moved_ref[where_ref[0] ^ (2 * k) ^ core] = ref[core]
    groups, _, rows, width = moved_ref.shape
    pairs = groups * rows // 2
    both = 2 * width
    sigma = jax.nn.sigmoid(gate_ref[...])

    def gather(get, block):
        low = [g for g in range(groups) if not g & block]
        first = jnp.concatenate([get(g) for g in low], axis=0)
        second = jnp.concatenate([get(g | block) for g in low], axis=0)
        return jnp.concatenate([first, second], axis=1)

    def scatter(put, value, block):
        low = [g for g in range(groups) if not g & block]
        for i, g in enumerate(low):
            piece = value[i * rows : (i + 1) * rows]
            put(g, piece[:, :width])
            put(g | block, piece[:, width:])

    for s, block in enumerate(blocks):
        source = moved_ref if s == 0 else back_ref
        joined = gather(lambda g: source[g, 0], block).astype(F32)
        centred = joined - jnp.mean(joined, axis=-1, keepdims=True)
        rstd = lax.rsqrt(jnp.mean(centred * centred, axis=-1, keepdims=True) + EPSILON)
        normed = centred * rstd
        low = normed.astype(BF16)
        here = pl.ds(s * pairs, pairs)
        normed_s[here, :] = normed
        joined_s[here, :] = joined
        low_s[here, :] = low
        rstd_s[here, :] = rstd
        preact = jnp.dot(low, we_ref[...], preferred_element_type=F32) + be_ref[...]
        hidden, slope = gelu_pair(preact)
        hidden = hidden.astype(BF16)
        hid_s[here, :] = hidden
        slope_s[here, :] = slope
        mixed = jnp.dot(hidden, wr_ref[...], preferred_element_type=F32)
        result = (sigma * joined + mixed + br_ref[...]).astype(BF16)

        def put(g, piece):
            back_ref[g, 0] = piece

        scatter(put, result, block)

    sum_be = jnp.zeros((1, we_ref.shape[1]), F32)
    sum_br = jnp.zeros((1, both), F32)
    sum_gate = jnp.zeros((1, both), F32)
    for s in reversed(range(len(blocks))):
        block = blocks[s]
        here = pl.ds(s * pairs, pairs)
        source = moved_ref if s == len(blocks) - 1 else back_ref
        gout = gather(lambda g: source[g, 1], block)
        gout_s[here, :] = gout
        gfloat = gout.astype(F32)
        sum_br += jnp.sum(gfloat, axis=0, keepdims=True)
        sum_gate += jnp.sum(gfloat * joined_s[here, :], axis=0, keepdims=True)
        ghidden = jnp.dot(gout, wrt_ref[...], preferred_element_type=F32)
        gpre = ghidden * slope_s[here, :]
        sum_be += jnp.sum(gpre, axis=0, keepdims=True)
        gpre = gpre.astype(BF16)
        gpre_s[here, :] = gpre
        gnormed = jnp.dot(gpre, wet_ref[...], preferred_element_type=F32)
        normed = normed_s[here, :]
        inner = gnormed - jnp.mean(gnormed, axis=-1, keepdims=True)
        inner = inner - normed * jnp.mean(gnormed * normed, axis=-1, keepdims=True)
        gjoined = (sigma * gfloat + rstd_s[here, :] * inner).astype(BF16)

        def put(g, piece):
            back_ref[g, 1] = piece

        scatter(put, gjoined, block)

    rows_t = (((0,), (0,)), ((), ()))
    acc_e[...] = lax.dot_general(low_s[...], gpre_s[...], rows_t, preferred_element_type=F32)
    acc_r[...] = lax.dot_general(hid_s[...], gout_s[...], rows_t, preferred_element_type=F32)

    me_ctx, me_rep = where_ref[0], where_ref[1]
    small = jnp.concatenate(
        [sum_be[:, :both], sum_be[:, both:], sum_br, sum_gate * sigma * (1.0 - sigma)], axis=0
    )
    for i, (order, parts, extra) in enumerate(chains):
        send, keep = messages[2 * i], messages[2 * i + 1]
        slabs = slabs_of(order, me_ctx, me_rep)
        half = len(slabs) // 2
        size = acc_r.shape[0] // len(slabs)
        for q, (shard, side) in enumerate(slabs):
            target = keep if q < half else send
            at = q % half * sum(count for _, _, count in parts)
            for name, start, count in parts:
                if name == "e":
                    row = pl.multiple_of(shard * size + start, math.gcd(size, start))
                    lane = pl.multiple_of(side * both, both)
                    value = acc_e[pl.ds(row, count), pl.ds(lane, both)]
                else:
                    row = pl.multiple_of((shard * 2 + side) * size + start, math.gcd(size, start))
                    value = acc_r[pl.ds(row, count), :]
                target[at : at + count, :] = value.astype(BF16)
                at += count
        if extra:
            write_extra((send, keep), small)


def halve_kernel(extra, keep_ref, recv_ref, send_out, keep_out):
    half = (keep_ref.shape[0] - extra) // 2
    for out, start in ((keep_out, 0), (send_out, half)):
        span = slice(start, start + half)
        out[:half, :] = (keep_ref[span, :].astype(F32) + recv_ref[span, :].astype(F32)).astype(BF16)
    if extra:
        write_extra((send_out, keep_out), read_extra(keep_ref, 4) + read_extra(recv_ref, 4))


def add_kernel(extra, keep_ref, recv_ref, out_ref, *bare_ref):
    size = keep_ref.shape[0] - extra
    total = (keep_ref[:size, :].astype(F32) + recv_ref[:size, :].astype(F32)).astype(BF16)
    for ref in (out_ref, *bare_ref):
        ref[:size, :] = total
    if extra:
        write_extra((out_ref,), read_extra(keep_ref, 4) + read_extra(recv_ref, 4))


def final_kernel(factor, chains, where_ref, *refs):
    owns, others, outs = refs[: len(chains)], refs[len(chains) : 2 * len(chains)], refs[2 * len(chains) :]
    out_e, out_be, out_r, out_br, out_gate = outs
    side = where_ref[1] & 1
    lanes = out_r.shape[1]
    size = out_r.shape[0] // 2
    for own, other, (_, parts, extra) in zip(owns, others, chains):
        for source, half in ((own, side), (other, 1 - side)):
            at = 0
            for name, start, count in parts:
                value = source[at : at + count, :].astype(F32) * factor
                at += count
                if name == "e":
                    out_e[start : start + count, pl.ds(pl.multiple_of(half * lanes, lanes), lanes)] = value
                else:
                    row = pl.multiple_of(half * size + start, math.gcd(size, start))
                    out_r[pl.ds(row, count), :] = value
        if extra:
            small = read_extra(own, 4) * factor
            out_be[:, :lanes] = small[0:1]
            out_be[:, lanes:] = small[1:2]
            out_br[...] = small[2:3]
            out_gate[...] = small[3:4]


VMEM = pl.BlockSpec(memory_space=pltpu.VMEM)
SMEM = pl.BlockSpec(memory_space=pltpu.SMEM)
HBM = pl.BlockSpec(memory_space=pltpu.HBM)


def call(kernel, name, shapes, args, scratch=(), scalars=0, flops=0, kind=VMEM, limit=32 * 2**10):
    size = sum(math.prod(a.shape) * a.dtype.itemsize for a in [*args, *shapes])
    return pl.pallas_call(
        kernel,
        name=name,
        out_shape=shapes,
        in_specs=[SMEM] * scalars + [kind] * (len(args) - scalars),
        out_specs=[VMEM] * len(shapes),
        scratch_shapes=scratch,
        cost_estimate=pl.CostEstimate(flops=flops, bytes_accessed=size, transcendentals=0),
        compiler_params=pltpu.CompilerParams(vmem_limit_bytes=limit * 2**10),
    )(*args)


def rows_of(count, lanes):
    return jax.ShapeDtypeStruct((count, lanes), BF16)


def add(extra, keep, got, bare):
    shapes = [rows_of(*keep.shape)]
    if bare and extra:
        shapes.append(rows_of(keep.shape[0] - extra, keep.shape[1]))
    outs = call(functools.partial(add_kernel, extra), "add", shapes, (keep, got))
    return outs[0], outs[-1]


def swap(value, axis, bit):
    return lax.ppermute(value, axis, [(i, i ^ bit) for i in range(lax.axis_size(axis))])


def body(inputs, w_expand, b_expand, w_reduce, b_reduce, gate_logit, cotangent):
    rows, width = inputs.shape[1:]
    devs, reps = lax.axis_size("ctx"), lax.axis_size("rep")
    slice_rows = rows // devs
    count = devs.bit_length() - 1
    groups = min(devs, 2**SECTIONS)
    inner = devs // groups
    blocks = [2 ** ((count - 1 - s) % count) // inner for s in range(SECTIONS)]
    both, hid = w_expand.shape

    ctx_bits = [("ctx", 2**i) for i in range(count)]
    rep_bits = [("rep", 2**i) for i in range(reps.bit_length() - 1)]
    size = both // devs
    later = ctx_bits[1:] + rep_bits[:1]
    if size % 64 == 0:
        cut = size * 3 // 4
        shares = [[("e", 0, cut)], [("r", 0, cut)], [("e", cut, size - cut), ("r", cut, size - cut)]]
    else:
        shares = [[("e", 0, size)], [("r", 0, size)]]
    chains = [
        (ctx_bits[:1] + later[i:] + later[:i], share, EXTRA * (i + 1 == len(shares))) for i, share in enumerate(shares)
    ]
    where = jnp.stack([lax.axis_index("ctx"), lax.axis_index("rep")]).astype(jnp.int32)

    like = jax.ShapeDtypeStruct
    state = like((groups, 2, inner * slice_rows, width), BF16)
    if devs == 8:
        part = like((devs // 2, 2, slice_rows, width), BF16)
        send, keep = call(
            pack_kernel, "pack", [part] * 2,
            (where, inputs.reshape(rows, width), cotangent.reshape(rows, width)),
            [pltpu.VMEM((rows, width), BF16)] * 2 + [pltpu.SemaphoreType.DMA((2,))], scalars=1, kind=HBM, limit=54912,
        )
        got = swap(send, "ctx", 1)
        relay = call(relay_kernel, "relay", [like((2,) + part.shape[1:], BF16)] * (devs // 2 - 1), (keep, got))
        arrived = [None] * len(relay)
        for k in reversed(range(len(relay))):
            arrived[k] = swap(relay[k], "ctx", 2 * (k + 1))
        arrived = [keep, got] + arrived
        moved_scratch = [pltpu.VMEM(state.shape, BF16)]
    else:
        packed = jnp.stack([a.reshape(devs, slice_rows, width) for a in (inputs, cotangent)], axis=1)
        moved = lax.all_to_all(packed, "ctx", split_axis=0, concat_axis=0, tiled=True)
        moved = moved.reshape(groups, inner, 2, slice_rows, width).swapaxes(1, 2)
        arrived = [moved.reshape(state.shape)]
        moved_scratch = []
    params = call(
        prep_kernel, "prep",
        [like((both, hid), BF16), like((hid, both), BF16), like((hid, both), BF16), like((both, hid), BF16)]
        + [like((1, hid), F32), like((1, both), F32), like((1, both), F32)],
        (w_expand, b_expand[None], w_reduce, b_reduce[None], gate_logit[None]),
        [pltpu.SemaphoreType.DMA((5,))], kind=HBM, limit=50432,
    )

    pairs = rows // 2
    total = SECTIONS * pairs
    slabs = 2 ** len(chains[0][0])
    messages = [
        rows_of(slabs // 2 * sum(n for _, _, n in parts) + extra, both) for _, parts, extra in chains for _ in range(2)
    ]
    back, *sums = call(
        functools.partial(main_kernel, blocks, chains, len(arrived)),
        "sections",
        [state] + messages,
        (where, *arrived, *params),
        [
            pltpu.VMEM((total, both), F32),
            pltpu.VMEM((total, both), BF16),
            pltpu.VMEM((total, hid), BF16),
            pltpu.VMEM((total, hid), F32),
            pltpu.VMEM((total, hid), BF16),
            pltpu.VMEM((total, both), BF16),
            pltpu.VMEM((total, 1), F32),
            pltpu.VMEM((total, both), F32),
            pltpu.VMEM((both, hid), F32),
            pltpu.VMEM((hid, both), F32),
        ]
        + moved_scratch,
        scalars=1,
        flops=12 * total * both * hid,
    )

    back = back.reshape(groups, 2, inner, slice_rows, width).swapaxes(1, 2).reshape(devs, 2, slice_rows, width)
    home = lax.all_to_all(back, "ctx", split_axis=0, concat_axis=0, tiled=True)
    outputs = home[:, 0].reshape(inputs.shape)
    grad_inputs = home[:, 1].reshape(inputs.shape)

    states = [(sums[2 * i], sums[2 * i + 1]) for i in range(len(chains))]
    steps = len(chains[0][0])
    for step in range(steps):
        got = [swap(send, *order[step]) for (send, _), (order, _, _) in zip(states, chains)]
        for i, (_, _, extra) in enumerate(chains):
            keep = states[i][1]
            if step + 1 < steps:
                count = (keep.shape[0] - extra) // 2 + extra
                states[i] = call(functools.partial(halve_kernel, extra), "halve", [rows_of(count, both)] * 2, (keep, got[i]))
            else:
                states[i] = add(extra, keep, got[i], len(rep_bits) == 1)
    for place, (axis, bit) in enumerate(rep_bits[1:]):
        got = [swap(own, axis, bit) for own, _ in states]
        for i, (_, _, extra) in enumerate(chains):
            states[i] = add(extra, states[i][0], got[i], place + 2 == len(rep_bits))
    others = [swap(bare, "rep", 1) for _, bare in states]
    factor = 1.0 / math.sqrt(reps * devs * rows)
    grad_e, grad_be, grad_r, grad_br, grad_gate = call(
        functools.partial(final_kernel, factor, chains),
        "final",
        [
            jax.ShapeDtypeStruct((both // devs, hid), F32),
            jax.ShapeDtypeStruct((1, hid), F32),
            jax.ShapeDtypeStruct((hid // devs, both), F32),
            jax.ShapeDtypeStruct((1, both), F32),
            jax.ShapeDtypeStruct((1, both), F32),
        ],
        (where, *[own for own, _ in states], *others),
        scalars=1,
    )
    return outputs, grad_inputs, grad_e, grad_be[0], grad_r, grad_br[0], grad_gate[0]


def solution(mesh):
    return jax.shard_map(
        body,
        mesh=mesh,
        in_specs=(P("rep", "ctx", None), P(), P(), P(), P(), P(), P("rep", "ctx", None)),
        out_specs=(
            P("rep", "ctx", None),
            P("rep", "ctx", None),
            P("ctx", None),
            P(),
            P("ctx", None),
            P(),
            P(),
        ),
        check_vma=False,
    )
```

```python
import functools
import math

import jax
import jax.numpy as jnp
from jax import lax
from jax.experimental import pallas as pl
from jax.experimental.pallas import tpu as pltpu
from jax.sharding import PartitionSpec as P

SECTIONS = 4
EPSILON = 1e-05
EXTRA = 16
F32 = jnp.float32
BF16 = jnp.bfloat16

ROOT = 0.3275911
COEFFS = (0.254829592, -0.284496736, 1.421413741, -1.453152027, 1.061405429)


def gelu_pair(x):
    bell = jnp.exp(-0.5 * x * x)
    t = 1.0 / (1.0 + (ROOT * math.sqrt(0.5)) * jnp.abs(x))
    poly = COEFFS[4]
    for a in (COEFFS[3], COEFFS[2], COEFFS[1], COEFFS[0]):
        poly = poly * t + a
    tail = (0.5 * poly * t) * bell
    cdf = jnp.where(x < 0.0, tail, 1.0 - tail)
    return x * cdf, cdf + x * bell * (1.0 / math.sqrt(2.0 * math.pi))


def split_parts(x):
    high = x.astype(BF16).astype(F32)
    return high, x - high


def write_extra(refs, small):
    high, low = split_parts(small)
    pad = jnp.zeros((EXTRA // 2 - small.shape[0], small.shape[1]), F32)
    rows = jnp.concatenate([high, pad, low, pad], axis=0).astype(BF16)
    for ref in refs:
        ref[ref.shape[0] - EXTRA :, :] = rows


def read_extra(ref, count):
    rows = ref[ref.shape[0] - EXTRA :, :].astype(F32)
    return rows[:count] + rows[EXTRA // 2 : EXTRA // 2 + count]


def slabs_of(orders, me_ctx, me_rep):
    steps = len(orders[0])
    slabs = []
    for q in range(2**steps):
        flips = []
        for order in orders:
            flip = {"ctx": 0, "rep": 0}
            for place, (axis, bit) in enumerate(order):
                if q >> (steps - 1 - place) & 1:
                    flip[axis] |= bit
            flips.append(flip)
        odd = (me_ctx & 1) ^ (q >> (steps - 1))
        ctx, rep = (flips[0][axis] + odd * (flips[1][axis] - flips[0][axis]) for axis in ("ctx", "rep"))
        slabs.append((me_ctx ^ ctx, (me_rep & 1) ^ rep))
    return slabs


def prep_kernel(we_ref, be_ref, wr_ref, br_ref, gate_ref, we_out, wet_out, wr_out, wrt_out, be_out, br_out, gate_out, sems):
    pairs = (
        (we_ref, we_out), (wr_ref, wr_out), (be_ref, be_out), (br_ref, br_out), (gate_ref, gate_out),
    )
    copies = [pltpu.make_async_copy(a, b, sems.at[i]) for i, (a, b) in enumerate(pairs)]
    for copy in copies:
        copy.start()
    copies[0].wait()
    wet_out[...] = we_out[...].T
    copies[1].wait()
    wrt_out[...] = wr_out[...].T
    for copy in copies[2:]:
        copy.wait()


def pack_kernel(where_ref, inputs_ref, cot_ref, send_ref, keep_ref, inputs_s, cot_s, sems):
    me = where_ref[0]
    chips, _, rows, _ = send_ref.shape
    sources = (inputs_s, cot_s)
    copies = [pltpu.make_async_copy(a, b, sems.at[i]) for i, (a, b) in enumerate(zip((inputs_ref, cot_ref), sources))]
    for copy in copies:
        copy.start()
    for which, source in enumerate(sources):
        copies[which].wait()
        for k in range(chips):
            for out, to in ((send_ref, me ^ (2 * k) ^ 1), (keep_ref, me ^ (2 * k))):
                out[k, which] = source[pl.ds(pl.multiple_of(to * rows, rows), rows), :]


def relay_kernel(keep_ref, got_ref, *outs):
    for k, out in enumerate(outs, 1):
        out[0] = keep_ref[k]
        out[1] = got_ref[k]


def main_kernel(blocks, chains, pieces, where_ref, *refs):
    arrived, refs = refs[:pieces], refs[pieces:]
    (
        we_ref, wet_ref, wr_ref, wrt_ref, be_ref, br_ref, gate_ref,
    ) = refs[:7]
    back_ref, messages, refs = refs[7], refs[8 : 8 + 2 * len(chains)], refs[8 + 2 * len(chains) :]
    (
        normed_s, low_s, hid_s, slope_s, gpre_s, gout_s, rstd_s, joined_s, acc_e, acc_r, sems, *moved_s,
    ) = refs
    state_s = moved_s[0]
    if pieces == 1:
        moved_ref = arrived[0]
    else:
        moved_ref = state_s
        keep_ref, got_ref, *relayed = arrived
        for core, ref in enumerate((keep_ref, got_ref)):
            moved_ref[where_ref[0] ^ core] = ref[0]
        for k, ref in enumerate(relayed, 1):
            for core in range(2):
                moved_ref[where_ref[0] ^ (2 * k) ^ core] = ref[core]
    groups, _, rows, width = moved_ref.shape
    pairs = groups * rows // 2
    both = 2 * width
    sigma = jax.nn.sigmoid(gate_ref[...])

    def gather(get, block):
        low = [g for g in range(groups) if not g & block]
        first = jnp.concatenate([get(g) for g in low], axis=0)
        second = jnp.concatenate([get(g | block) for g in low], axis=0)
        return jnp.concatenate([first, second], axis=1)

    def scatter(put, value, block):
        low = [g for g in range(groups) if not g & block]
        for i, g in enumerate(low):
            piece = value[i * rows : (i + 1) * rows]
            put(g, piece[:, :width])
            put(g | block, piece[:, width:])

    for s, block in enumerate(blocks):
        source = moved_ref if s == 0 else state_s
        joined = gather(lambda g: source[g, 0], block).astype(F32)
        centred = joined - jnp.mean(joined, axis=-1, keepdims=True)
        rstd = lax.rsqrt(jnp.mean(centred * centred, axis=-1, keepdims=True) + EPSILON)
        normed = centred * rstd
        low = normed.astype(BF16)
        here = pl.ds(s * pairs, pairs)
        normed_s[here, :] = normed
        joined_s[here, :] = joined
        low_s[here, :] = low
        rstd_s[here, :] = rstd
        preact = jnp.dot(low, we_ref[...], preferred_element_type=F32) + be_ref[...]
        hidden, slope = gelu_pair(preact)
        hidden = hidden.astype(BF16)
        hid_s[here, :] = hidden
        slope_s[here, :] = slope
        mixed = jnp.dot(hidden, wr_ref[...], preferred_element_type=F32)
        result = (sigma * joined + mixed + br_ref[...]).astype(BF16)

        def put(g, piece):
            state_s[g, 0] = piece

        scatter(put, result, block)

    copies = [pltpu.make_async_copy(state_s.at[:, i], back_ref.at[:, i], sems.at[i]) for i in range(2)]
    copies[0].start()
    sum_be = jnp.zeros((1, we_ref.shape[1]), F32)
    sum_br = jnp.zeros((1, both), F32)
    sum_gate = jnp.zeros((1, both), F32)
    for s in reversed(range(len(blocks))):
        block = blocks[s]
        here = pl.ds(s * pairs, pairs)
        source = moved_ref if s == len(blocks) - 1 else state_s
        gout = gather(lambda g: source[g, 1], block)
        gout_s[here, :] = gout
        gfloat = gout.astype(F32)
        sum_br += jnp.sum(gfloat, axis=0, keepdims=True)
        sum_gate += jnp.sum(gfloat * joined_s[here, :], axis=0, keepdims=True)
        ghidden = jnp.dot(gout, wrt_ref[...], preferred_element_type=F32)
        gpre = ghidden * slope_s[here, :]
        sum_be += jnp.sum(gpre, axis=0, keepdims=True)
        gpre = gpre.astype(BF16)
        gpre_s[here, :] = gpre
        gnormed = jnp.dot(gpre, wet_ref[...], preferred_element_type=F32)
        normed = normed_s[here, :]
        inner = gnormed - jnp.mean(gnormed, axis=-1, keepdims=True)
        inner = inner - normed * jnp.mean(gnormed * normed, axis=-1, keepdims=True)
        gjoined = (sigma * gfloat + rstd_s[here, :] * inner).astype(BF16)

        def put(g, piece):
            state_s[g, 1] = piece

        scatter(put, gjoined, block)

    copies[1].start()
    rows_t = (((0,), (0,)), ((), ()))
    acc_e[...] = lax.dot_general(low_s[...], gpre_s[...], rows_t, preferred_element_type=F32)
    acc_r[...] = lax.dot_general(hid_s[...], gout_s[...], rows_t, preferred_element_type=F32)

    me_ctx, me_rep = where_ref[0], where_ref[1]
    small = jnp.concatenate(
        [sum_be[:, :both], sum_be[:, both:], sum_br, sum_gate * sigma * (1.0 - sigma)], axis=0
    )
    for i, (orders, parts, extra) in enumerate(chains):
        send, keep = messages[2 * i], messages[2 * i + 1]
        slabs = slabs_of(orders, me_ctx, me_rep)
        half = len(slabs) // 2
        size = acc_r.shape[0] // len(slabs)
        for q, (shard, side) in enumerate(slabs):
            target = keep if q < half else send
            at = q % half * sum(count for _, _, count in parts)
            for name, start, count in parts:
                if name == "e":
                    row = pl.multiple_of(shard * size + start, math.gcd(size, start))
                    lane = pl.multiple_of(side * both, both)
                    value = acc_e[pl.ds(row, count), pl.ds(lane, both)]
                else:
                    row = pl.multiple_of((shard * 2 + side) * size + start, math.gcd(size, start))
                    value = acc_r[pl.ds(row, count), :]
                target[at : at + count, :] = value.astype(BF16)
                at += count
        if extra:
            write_extra((send, keep), small)
    for copy in copies:
        copy.wait()


def halve_kernel(extra, keep_ref, recv_ref, *refs):
    send_out, keep_out = refs[-2:]
    half = (keep_ref.shape[0] - extra) // 2
    for out, start in ((keep_out, 0), (send_out, half)):
        span = slice(start, start + half)
        out[:half, :] = (keep_ref[span, :].astype(F32) + recv_ref[span, :].astype(F32)).astype(BF16)
    if extra:
        write_extra((send_out, keep_out), read_extra(keep_ref, 4) + read_extra(recv_ref, 4))


def add_kernel(extra, keep_ref, recv_ref, out_ref, *bare_ref):
    size = keep_ref.shape[0] - extra
    total = (keep_ref[:size, :].astype(F32) + recv_ref[:size, :].astype(F32)).astype(BF16)
    for ref in (out_ref, *bare_ref):
        ref[:size, :] = total
    if extra:
        write_extra((out_ref,), read_extra(keep_ref, 4) + read_extra(recv_ref, 4))


def final_kernel(factor, chains, where_ref, *refs):
    owns, others, outs = refs[: len(chains)], refs[len(chains) : 2 * len(chains)], refs[2 * len(chains) :]
    out_e, out_be, out_r, out_br, out_gate = outs
    side = where_ref[1] & 1
    lanes = out_r.shape[1]
    size = out_r.shape[0] // 2
    for own, other, (_, parts, extra) in zip(owns, others, chains):
        for source, half in ((own, side), (other, 1 - side)):
            at = 0
            for name, start, count in parts:
                value = source[at : at + count, :].astype(F32) * factor
                at += count
                if name == "e":
                    out_e[start : start + count, pl.ds(pl.multiple_of(half * lanes, lanes), lanes)] = value
                else:
                    row = pl.multiple_of(half * size + start, math.gcd(size, start))
                    out_r[pl.ds(row, count), :] = value
        if extra:
            small = read_extra(own, 4) * factor
            out_be[:, :lanes] = small[0:1]
            out_be[:, lanes:] = small[1:2]
            out_br[...] = small[2:3]
            out_gate[...] = small[3:4]


VMEM = pl.BlockSpec(memory_space=pltpu.VMEM)
SMEM = pl.BlockSpec(memory_space=pltpu.SMEM)
HBM = pl.BlockSpec(memory_space=pltpu.HBM)


def call(kernel, name, shapes, args, scratch=(), scalars=0, flops=0, kind=VMEM, limit=32 * 2**10, far=0):
    size = sum(math.prod(a.shape) * a.dtype.itemsize for a in [*args, *shapes])
    return pl.pallas_call(
        kernel,
        name=name,
        out_shape=shapes,
        in_specs=[SMEM] * scalars + [kind] * (len(args) - scalars),
        out_specs=[HBM] * far + [VMEM] * (len(shapes) - far),
        scratch_shapes=scratch,
        cost_estimate=pl.CostEstimate(flops=flops, bytes_accessed=size, transcendentals=0),
        compiler_params=pltpu.CompilerParams(vmem_limit_bytes=limit * 2**10),
    )(*args)


def rows_of(count, lanes):
    return jax.ShapeDtypeStruct((count, lanes), BF16)


def add(extra, keep, got, bare):
    shapes = [rows_of(*keep.shape)]
    if bare and extra:
        shapes.append(rows_of(keep.shape[0] - extra, keep.shape[1]))
    outs = call(functools.partial(add_kernel, extra), "add", shapes, (keep, got))
    return outs[0], outs[-1]


def swap(value, axis, bit):
    return lax.ppermute(value, axis, [(i, i ^ bit) for i in range(lax.axis_size(axis))])


def swap_by_place(value, bits):
    devs, reps = lax.axis_size("ctx"), lax.axis_size("rep")
    pairs = []
    for c in range(devs):
        axis, bit = bits[c & 1]
        for r in range(reps):
            to = (c ^ bit, r) if axis == "ctx" else (c, r ^ bit)
            pairs.append((c * reps + r, to[0] * reps + to[1]))
    return lax.ppermute(value, ("ctx", "rep"), pairs)


def body(inputs, w_expand, b_expand, w_reduce, b_reduce, gate_logit, cotangent):
    rows, width = inputs.shape[1:]
    devs, reps = lax.axis_size("ctx"), lax.axis_size("rep")
    slice_rows = rows // devs
    count = devs.bit_length() - 1
    groups = min(devs, 2**SECTIONS)
    inner = devs // groups
    blocks = [2 ** ((count - 1 - s) % count) // inner for s in range(SECTIONS)]
    both, hid = w_expand.shape

    ctx_bits = [("ctx", 2**i) for i in range(count)]
    rep_bits = [("rep", 2**i) for i in range(reps.bit_length() - 1)]
    size = both // devs
    later = ctx_bits[1:] + rep_bits[:1]
    if size % 64 == 0:
        cut, most = size // 2, size * 3 // 4
        shares = [[("e", 0, cut)], [("r", 0, most)], [("e", cut, size - cut), ("r", most, size - most)]]
    else:
        shares = [[("e", 0, size)], [("r", 0, size)]]
    turns = [(0, 0), (1, 1), (2, 2)]
    chains = [
        (tuple(ctx_bits[:1] + later[turn:] + later[:turn] for turn in pair), share, extra)
        for pair, share, extra in zip(turns, shares, (EXTRA, 0, 0))
    ]
    where = jnp.stack([lax.axis_index("ctx"), lax.axis_index("rep")]).astype(jnp.int32)

    like = jax.ShapeDtypeStruct
    state = like((groups, 2, inner * slice_rows, width), BF16)
    if devs == 8:
        part = like((devs // 2, 2, slice_rows, width), BF16)
        send, keep = call(
            pack_kernel, "pack", [part] * 2,
            (where, inputs.reshape(rows, width), cotangent.reshape(rows, width)),
            [pltpu.VMEM((rows, width), BF16)] * 2 + [pltpu.SemaphoreType.DMA((2,))], scalars=1, kind=HBM, limit=54912,
        )
        got = swap(send, "ctx", 1)
        relay = call(relay_kernel, "relay", [like((2,) + part.shape[1:], BF16)] * (devs // 2 - 1), (keep, got))
        arrived = [None] * len(relay)
        for k in reversed(range(len(relay))):
            arrived[k] = swap(relay[k], "ctx", 2 * (k + 1))
        arrived = [keep, got] + arrived
        moved_scratch = [pltpu.VMEM(state.shape, BF16)]
    else:
        packed = jnp.stack([a.reshape(devs, slice_rows, width) for a in (inputs, cotangent)], axis=1)
        moved = lax.all_to_all(packed, "ctx", split_axis=0, concat_axis=0, tiled=True)
        moved = moved.reshape(groups, inner, 2, slice_rows, width).swapaxes(1, 2)
        arrived = [moved.reshape(state.shape)]
        moved_scratch = [pltpu.VMEM(state.shape, BF16)]
    params = call(
        prep_kernel, "prep",
        [like((both, hid), BF16), like((hid, both), BF16), like((hid, both), BF16), like((both, hid), BF16)]
        + [like((1, hid), F32), like((1, both), F32), like((1, both), F32)],
        (w_expand, b_expand[None], w_reduce, b_reduce[None], gate_logit[None]),
        [pltpu.SemaphoreType.DMA((5,))], kind=HBM, limit=50432,
    )

    pairs = rows // 2
    total = SECTIONS * pairs
    slabs = 2 ** len(chains[0][0][0])
    messages = [
        rows_of(slabs // 2 * sum(n for _, _, n in parts) + extra, both) for _, parts, extra in chains for _ in range(2)
    ]
    back, *sums = call(
        functools.partial(main_kernel, blocks, chains, len(arrived)),
        "sections",
        [state] + messages,
        (where, *arrived, *params),
        [
            pltpu.VMEM((total, both), F32),
            pltpu.VMEM((total, both), BF16),
            pltpu.VMEM((total, hid), BF16),
            pltpu.VMEM((total, hid), F32),
            pltpu.VMEM((total, hid), BF16),
            pltpu.VMEM((total, both), BF16),
            pltpu.VMEM((total, 1), F32),
            pltpu.VMEM((total, both), F32),
            pltpu.VMEM((both, hid), F32),
            pltpu.VMEM((hid, both), F32),
            pltpu.SemaphoreType.DMA((2,)),
        ]
        + moved_scratch,
        scalars=1,
        far=1,
        flops=12 * total * both * hid,
    )

    home = None

    def place(point, sends):
        nonlocal back, home
        if point == 1:
            if False: sends, back = lax.optimization_barrier((sends, back))
            back = back.reshape(groups, 2, inner, slice_rows, width).swapaxes(1, 2)
            back = back.reshape(devs, 2, slice_rows, width)
            home = lax.all_to_all(back, "ctx", split_axis=0, concat_axis=0, tiled=True)
        if point == 0:
            last, home = lax.optimization_barrier((sends[-1], home))
            sends = sends[:-1] + [last]
        return sends

    states = [(sums[2 * i], sums[2 * i + 1]) for i in range(len(chains))]
    steps = len(chains[0][0][0])
    for step in range(steps):
        got = [swap_by_place(send, [order[step] for order in orders]) for send, (orders, _, _) in zip(place(step, [s for s, _ in states]), chains)]
        for i, (_, _, extra) in enumerate(chains):
            keep = states[i][1]
            after = [states[i - 1][0]] if i and step in (1, 2) else []
            if step + 1 < steps:
                count = (keep.shape[0] - extra) // 2 + extra
                states[i] = call(functools.partial(halve_kernel, extra), "halve", [rows_of(count, both)] * 2, (keep, got[i], *after))
            else:
                states[i] = add(extra, keep, got[i], len(rep_bits) == 1)
    for place, (axis, bit) in enumerate(rep_bits[1:]):
        got = [swap(own, axis, bit) for own, _ in states]
        for i, (_, _, extra) in enumerate(chains):
            states[i] = add(extra, states[i][0], got[i], place + 2 == len(rep_bits))
    others = [swap(bare, "rep", 1) for _, bare in states]
    outputs, grad_inputs = (home[:, i].reshape(inputs.shape) for i in range(2))
    factor = 1.0 / math.sqrt(reps * devs * rows)
    grad_e, grad_be, grad_r, grad_br, grad_gate = call(
        functools.partial(final_kernel, factor, chains),
        "final",
        [
            jax.ShapeDtypeStruct((both // devs, hid), F32),
            jax.ShapeDtypeStruct((1, hid), F32),
            jax.ShapeDtypeStruct((hid // devs, both), F32),
            jax.ShapeDtypeStruct((1, both), F32),
            jax.ShapeDtypeStruct((1, both), F32),
        ],
        (where, *[own for own, _ in states], *others),
        scalars=1,
    )
    return outputs, grad_inputs, grad_e, grad_be[0], grad_r, grad_br[0], grad_gate[0]


def solution(mesh):
    return jax.shard_map(
        body,
        mesh=mesh,
        in_specs=(P("rep", "ctx", None), P(), P(), P(), P(), P(), P("rep", "ctx", None)),
        out_specs=(
            P("rep", "ctx", None),
            P("rep", "ctx", None),
            P("ctx", None),
            P(),
            P("ctx", None),
            P(),
            P(),
        ),
        check_vma=False,
    )
```

```python
import functools
import math

import jax
import jax.numpy as jnp
from jax import lax
from jax.experimental import pallas as pl
from jax.experimental.pallas import tpu as pltpu
from jax.sharding import PartitionSpec as P

SECTIONS = 4
EPSILON = 1e-05
EXTRA = 16
F32 = jnp.float32
BF16 = jnp.bfloat16

ROOT = 0.3275911
COEFFS = (0.254829592, -0.284496736, 1.421413741, -1.453152027, 1.061405429)


def gelu_pair(x):
    bell = jnp.exp(-0.5 * x * x)
    t = 1.0 / (1.0 + (ROOT * math.sqrt(0.5)) * jnp.abs(x))
    poly = COEFFS[4]
    for a in (COEFFS[3], COEFFS[2], COEFFS[1], COEFFS[0]):
        poly = poly * t + a
    tail = (0.5 * poly * t) * bell
    cdf = jnp.where(x < 0.0, tail, 1.0 - tail)
    return x * cdf, cdf + x * bell * (1.0 / math.sqrt(2.0 * math.pi))


def split_parts(x):
    high = x.astype(BF16).astype(F32)
    return high, x - high


def write_extra(refs, small):
    high, low = split_parts(small)
    pad = jnp.zeros((EXTRA // 2 - small.shape[0], small.shape[1]), F32)
    rows = jnp.concatenate([high, pad, low, pad], axis=0).astype(BF16)
    for ref in refs:
        ref[ref.shape[0] - EXTRA :, :] = rows


def read_extra(ref, count):
    rows = ref[ref.shape[0] - EXTRA :, :].astype(F32)
    return rows[:count] + rows[EXTRA // 2 : EXTRA // 2 + count]


def slabs_of(orders, me_ctx, me_rep):
    steps = len(orders[0])
    slabs = []
    for q in range(2**steps):
        flips = []
        for order in orders:
            flip = {"ctx": 0, "rep": 0}
            for place, (axis, bit) in enumerate(order):
                if q >> (steps - 1 - place) & 1:
                    flip[axis] |= bit
            flips.append(flip)
        odd = (me_ctx & 1) ^ (q >> (steps - 1))
        ctx, rep = (flips[0][axis] + odd * (flips[1][axis] - flips[0][axis]) for axis in ("ctx", "rep"))
        slabs.append((me_ctx ^ ctx, (me_rep & 1) ^ rep))
    return slabs


def prep_kernel(we_ref, be_ref, wr_ref, br_ref, gate_ref, we_out, wet_out, wr_out, wrt_out, be_out, br_out, gate_out, sems):
    pairs = (
        (we_ref, we_out), (wr_ref, wr_out), (be_ref, be_out), (br_ref, br_out), (gate_ref, gate_out),
    )
    copies = [pltpu.make_async_copy(a, b, sems.at[i]) for i, (a, b) in enumerate(pairs)]
    for copy in copies:
        copy.start()
    copies[0].wait()
    wet_out[...] = we_out[...].T
    copies[1].wait()
    wrt_out[...] = wr_out[...].T
    for copy in copies[2:]:
        copy.wait()


def pack_kernel(where_ref, inputs_ref, cot_ref, send_ref, keep_ref, inputs_s, cot_s, sems):
    me = where_ref[0]
    chips, _, rows, _ = send_ref.shape
    sources = (inputs_s, cot_s)
    copies = [pltpu.make_async_copy(a, b, sems.at[i]) for i, (a, b) in enumerate(zip((inputs_ref, cot_ref), sources))]
    for copy in copies:
        copy.start()
    for which, source in enumerate(sources):
        copies[which].wait()
        for k in range(chips):
            for out, to in ((send_ref, me ^ (2 * k) ^ 1), (keep_ref, me ^ (2 * k))):
                out[k, which] = source[pl.ds(pl.multiple_of(to * rows, rows), rows), :]


def relay_kernel(keep_ref, got_ref, *outs):
    for k, out in enumerate(outs, 1):
        out[0] = keep_ref[k]
        out[1] = got_ref[k]


def main_kernel(blocks, chains, pieces, where_ref, *refs):
    arrived, refs = refs[:pieces], refs[pieces:]
    (
        we_ref, wet_ref, wr_ref, wrt_ref, be_ref, br_ref, gate_ref,
    ) = refs[:7]
    back_ref, messages, refs = refs[7], refs[8 : 8 + 2 * len(chains)], refs[8 + 2 * len(chains) :]
    (
        normed_s, low_s, hid_s, slope_s, gpre_s, gout_s, rstd_s, joined_s, acc_e, acc_r, sems, *moved_s,
    ) = refs
    state_s = moved_s[0]
    if pieces == 1:
        moved_ref = arrived[0]
    else:
        moved_ref = state_s
        keep_ref, got_ref, *relayed = arrived
        for core, ref in enumerate((keep_ref, got_ref)):
            moved_ref[where_ref[0] ^ core] = ref[0]
        for k, ref in enumerate(relayed, 1):
            for core in range(2):
                moved_ref[where_ref[0] ^ (2 * k) ^ core] = ref[core]
    groups, _, rows, width = moved_ref.shape
    pairs = groups * rows // 2
    both = 2 * width
    sigma = jax.nn.sigmoid(gate_ref[...])

    def gather(get, block):
        low = [g for g in range(groups) if not g & block]
        first = jnp.concatenate([get(g) for g in low], axis=0)
        second = jnp.concatenate([get(g | block) for g in low], axis=0)
        return jnp.concatenate([first, second], axis=1)

    def scatter(put, value, block):
        low = [g for g in range(groups) if not g & block]
        for i, g in enumerate(low):
            piece = value[i * rows : (i + 1) * rows]
            put(g, piece[:, :width])
            put(g | block, piece[:, width:])

    for s, block in enumerate(blocks):
        source = moved_ref if s == 0 else state_s
        joined = gather(lambda g: source[g, 0], block).astype(F32)
        centred = joined - jnp.mean(joined, axis=-1, keepdims=True)
        rstd = lax.rsqrt(jnp.mean(centred * centred, axis=-1, keepdims=True) + EPSILON)
        normed = centred * rstd
        low = normed.astype(BF16)
        here = pl.ds(s * pairs, pairs)
        normed_s[here, :] = normed
        joined_s[here, :] = joined
        low_s[here, :] = low
        rstd_s[here, :] = rstd
        preact = jnp.dot(low, we_ref[...], preferred_element_type=F32) + be_ref[...]
        hidden, slope = gelu_pair(preact)
        hidden = hidden.astype(BF16)
        hid_s[here, :] = hidden
        slope_s[here, :] = slope
        mixed = jnp.dot(hidden, wr_ref[...], preferred_element_type=F32)
        result = (sigma * joined + mixed + br_ref[...]).astype(BF16)

        def put(g, piece):
            state_s[g, 0] = piece

        scatter(put, result, block)

    copies = [pltpu.make_async_copy(state_s.at[:, i], back_ref.at[:, i], sems.at[i]) for i in range(2)]
    copies[0].start()
    sum_be = jnp.zeros((1, we_ref.shape[1]), F32)
    sum_br = jnp.zeros((1, both), F32)
    sum_gate = jnp.zeros((1, both), F32)
    for s in reversed(range(len(blocks))):
        block = blocks[s]
        here = pl.ds(s * pairs, pairs)
        source = moved_ref if s == len(blocks) - 1 else state_s
        gout = gather(lambda g: source[g, 1], block)
        gout_s[here, :] = gout
        gfloat = gout.astype(F32)
        sum_br += jnp.sum(gfloat, axis=0, keepdims=True)
        sum_gate += jnp.sum(gfloat * joined_s[here, :], axis=0, keepdims=True)
        ghidden = jnp.dot(gout, wrt_ref[...], preferred_element_type=F32)
        gpre = ghidden * slope_s[here, :]
        sum_be += jnp.sum(gpre, axis=0, keepdims=True)
        gpre = gpre.astype(BF16)
        gpre_s[here, :] = gpre
        gnormed = jnp.dot(gpre, wet_ref[...], preferred_element_type=F32)
        normed = normed_s[here, :]
        inner = gnormed - jnp.mean(gnormed, axis=-1, keepdims=True)
        inner = inner - normed * jnp.mean(gnormed * normed, axis=-1, keepdims=True)
        gjoined = (sigma * gfloat + rstd_s[here, :] * inner).astype(BF16)

        def put(g, piece):
            state_s[g, 1] = piece

        scatter(put, gjoined, block)

    copies[1].start()
    rows_t = (((0,), (0,)), ((), ()))
    acc_e[...] = lax.dot_general(low_s[...], gpre_s[...], rows_t, preferred_element_type=F32)
    acc_r[...] = lax.dot_general(hid_s[...], gout_s[...], rows_t, preferred_element_type=F32)

    me_ctx, me_rep = where_ref[0], where_ref[1]
    small = jnp.concatenate(
        [sum_be[:, :both], sum_be[:, both:], sum_br, sum_gate * sigma * (1.0 - sigma)], axis=0
    )
    for i, (orders, parts, extra) in enumerate(chains):
        send, keep = messages[2 * i], messages[2 * i + 1]
        slabs = slabs_of(orders, me_ctx, me_rep)
        half = len(slabs) // 2
        size = acc_r.shape[0] // len(slabs)
        for q, (shard, side) in enumerate(slabs):
            target = keep if q < half else send
            at = q % half * sum(count for _, _, count in parts)
            for name, start, count in parts:
                if name == "e":
                    row = pl.multiple_of(shard * size + start, math.gcd(size, start))
                    lane = pl.multiple_of(side * both, both)
                    value = acc_e[pl.ds(row, count), pl.ds(lane, both)]
                else:
                    row = pl.multiple_of((shard * 2 + side) * size + start, math.gcd(size, start))
                    value = acc_r[pl.ds(row, count), :]
                target[at : at + count, :] = value.astype(BF16)
                at += count
        if extra:
            write_extra((send, keep), small)
    for copy in copies:
        copy.wait()


def halve_kernel(extra, keep_ref, recv_ref, *refs):
    send_out, keep_out = refs[-2:]
    half = (keep_ref.shape[0] - extra) // 2
    for out, start in ((keep_out, 0), (send_out, half)):
        span = slice(start, start + half)
        out[:half, :] = (keep_ref[span, :].astype(F32) + recv_ref[span, :].astype(F32)).astype(BF16)
    if extra:
        write_extra((send_out, keep_out), read_extra(keep_ref, 4) + read_extra(recv_ref, 4))


def add_kernel(extra, count, *refs):
    kept, got, outs = refs[:count], refs[count : 2 * count], refs[2 * count :]
    at = 0
    for i, (keep_ref, recv_ref) in enumerate(zip(kept, got)):
        size = keep_ref.shape[0] - (0 if i else extra)
        total = (keep_ref[:size, :].astype(F32) + recv_ref[:size, :].astype(F32)).astype(BF16)
        for ref in outs:
            ref[at : at + size, :] = total
        at += size
    if extra:
        write_extra(outs[:1], read_extra(kept[0], 4) + read_extra(got[0], 4))


def final_kernel(factor, chains, where_ref, *refs):
    owns, others, outs = refs[: len(chains)], refs[len(chains) : 2 * len(chains)], refs[2 * len(chains) :]
    out_e, out_be, out_r, out_br, out_gate = outs
    side = where_ref[1] & 1
    lanes = out_r.shape[1]
    size = out_r.shape[0] // 2
    for own, other, (_, parts, extra) in zip(owns, others, chains):
        for source, half in ((own, side), (other, 1 - side)):
            at = 0
            for name, start, count in parts:
                value = source[at : at + count, :].astype(F32) * factor
                at += count
                if name == "e":
                    out_e[start : start + count, pl.ds(pl.multiple_of(half * lanes, lanes), lanes)] = value
                else:
                    row = pl.multiple_of(half * size + start, math.gcd(size, start))
                    out_r[pl.ds(row, count), :] = value
        if extra:
            small = read_extra(own, 4) * factor
            out_be[:, :lanes] = small[0:1]
            out_be[:, lanes:] = small[1:2]
            out_br[...] = small[2:3]
            out_gate[...] = small[3:4]


VMEM = pl.BlockSpec(memory_space=pltpu.VMEM)
SMEM = pl.BlockSpec(memory_space=pltpu.SMEM)
HBM = pl.BlockSpec(memory_space=pltpu.HBM)


def call(kernel, name, shapes, args, scratch=(), scalars=0, flops=0, kind=VMEM, limit=32 * 2**10, far=0):
    size = sum(math.prod(a.shape) * a.dtype.itemsize for a in [*args, *shapes])
    return pl.pallas_call(
        kernel,
        name=name,
        out_shape=shapes,
        in_specs=[SMEM] * scalars + [kind] * (len(args) - scalars),
        out_specs=[HBM] * far + [VMEM] * (len(shapes) - far),
        scratch_shapes=scratch,
        cost_estimate=pl.CostEstimate(flops=flops, bytes_accessed=size, transcendentals=0),
        compiler_params=pltpu.CompilerParams(vmem_limit_bytes=limit * 2**10),
    )(*args)


def rows_of(count, lanes):
    return jax.ShapeDtypeStruct((count, lanes), BF16)


def add(extra, kept, got, bare):
    size = sum(keep.shape[0] for keep in kept)
    shapes = [rows_of(size, kept[0].shape[1])]
    if bare and extra:
        shapes.append(rows_of(size - extra, kept[0].shape[1]))
    outs = call(functools.partial(add_kernel, extra, len(kept)), "add", shapes, (*kept, *got))
    return outs[0], outs[-1]


def swap(value, axis, bit):
    return lax.ppermute(value, axis, [(i, i ^ bit) for i in range(lax.axis_size(axis))])


def swap_by_place(value, bits):
    devs, reps = lax.axis_size("ctx"), lax.axis_size("rep")
    pairs = []
    for c in range(devs):
        axis, bit = bits[c & 1]
        for r in range(reps):
            to = (c ^ bit, r) if axis == "ctx" else (c, r ^ bit)
            pairs.append((c * reps + r, to[0] * reps + to[1]))
    return lax.ppermute(value, ("ctx", "rep"), pairs)


def body(inputs, w_expand, b_expand, w_reduce, b_reduce, gate_logit, cotangent):
    rows, width = inputs.shape[1:]
    devs, reps = lax.axis_size("ctx"), lax.axis_size("rep")
    slice_rows = rows // devs
    count = devs.bit_length() - 1
    groups = min(devs, 2**SECTIONS)
    inner = devs // groups
    blocks = [2 ** ((count - 1 - s) % count) // inner for s in range(SECTIONS)]
    both, hid = w_expand.shape

    ctx_bits = [("ctx", 2**i) for i in range(count)]
    rep_bits = [("rep", 2**i) for i in range(reps.bit_length() - 1)]
    size = both // devs
    later = (ctx_bits[1:] + rep_bits[:1])[::-1]
    if size % 64 == 0:
        cut = size * 3 // 4
        shares = [[("e", 0, cut)], [("r", 0, cut)], [("e", cut, size - cut), ("r", cut, size - cut)]]
    else:
        shares = [[("e", 0, size)], [("r", 0, size)]]
    chains = [
        ((ctx_bits[:1] + later[turn:] + later[:turn],) * 2, share, EXTRA * (turn == 0))
        for turn, share in zip(reversed(range(len(shares))), shares)
    ]
    where = jnp.stack([lax.axis_index("ctx"), lax.axis_index("rep")]).astype(jnp.int32)

    like = jax.ShapeDtypeStruct
    state = like((groups, 2, inner * slice_rows, width), BF16)
    if devs == 8:
        part = like((devs // 2, 2, slice_rows, width), BF16)
        send, keep = call(
            pack_kernel, "pack", [part] * 2,
            (where, inputs.reshape(rows, width), cotangent.reshape(rows, width)),
            [pltpu.VMEM((rows, width), BF16)] * 2 + [pltpu.SemaphoreType.DMA((2,))], scalars=1, kind=HBM, limit=54912,
        )
        got = swap(send, "ctx", 1)
        relay = call(relay_kernel, "relay", [like((2,) + part.shape[1:], BF16)] * (devs // 2 - 1), (keep, got))
        arrived = [None] * len(relay)
        for k in reversed(range(len(relay))):
            arrived[k] = swap(relay[k], "ctx", 2 * (k + 1))
        arrived = [keep, got] + arrived
        moved_scratch = [pltpu.VMEM(state.shape, BF16)]
    else:
        packed = jnp.stack([a.reshape(devs, slice_rows, width) for a in (inputs, cotangent)], axis=1)
        moved = lax.all_to_all(packed, "ctx", split_axis=0, concat_axis=0, tiled=True)
        moved = moved.reshape(groups, inner, 2, slice_rows, width).swapaxes(1, 2)
        arrived = [moved.reshape(state.shape)]
        moved_scratch = [pltpu.VMEM(state.shape, BF16)]
    params = call(
        prep_kernel, "prep",
        [like((both, hid), BF16), like((hid, both), BF16), like((hid, both), BF16), like((both, hid), BF16)]
        + [like((1, hid), F32), like((1, both), F32), like((1, both), F32)],
        (w_expand, b_expand[None], w_reduce, b_reduce[None], gate_logit[None]),
        [pltpu.SemaphoreType.DMA((5,))], kind=HBM, limit=50432,
    )

    pairs = rows // 2
    total = SECTIONS * pairs
    slabs = 2 ** len(chains[0][0][0])
    messages = [
        rows_of(slabs // 2 * sum(n for _, _, n in parts) + extra, both) for _, parts, extra in chains for _ in range(2)
    ]
    back, *sums = call(
        functools.partial(main_kernel, blocks, chains, len(arrived)),
        "sections",
        [state] + messages,
        (where, *arrived, *params),
        [
            pltpu.VMEM((total, both), F32),
            pltpu.VMEM((total, both), BF16),
            pltpu.VMEM((total, hid), BF16),
            pltpu.VMEM((total, hid), F32),
            pltpu.VMEM((total, hid), BF16),
            pltpu.VMEM((total, both), BF16),
            pltpu.VMEM((total, 1), F32),
            pltpu.VMEM((total, both), F32),
            pltpu.VMEM((both, hid), F32),
            pltpu.VMEM((hid, both), F32),
            pltpu.SemaphoreType.DMA((2,)),
        ]
        + moved_scratch,
        scalars=1,
        far=1,
        flops=12 * total * both * hid,
    )

    back = back.reshape(groups, 2, inner, slice_rows, width).swapaxes(1, 2)
    home = lax.all_to_all(back.reshape(devs, 2, slice_rows, width), "ctx", split_axis=0, concat_axis=0, tiled=True)

    states = [(sums[2 * i], sums[2 * i + 1]) for i in range(len(chains))]
    steps = len(chains[0][0][0])
    for step in range(steps):
        got = [
            swap_by_place(send, [order[step] for order in orders]) for (send, _), (orders, _, _) in zip(states, chains)
        ]
        if step + 1 == steps:
            break
        for i, (_, _, extra) in enumerate(chains):
            keep = states[i][1]
            after = [states[i - 1][0]] if i and step else []
            count = (keep.shape[0] - extra) // 2 + extra
            states[i] = call(
                functools.partial(halve_kernel, extra), "halve", [rows_of(count, both)] * 2, (keep, got[i], *after)
            )
    joined = [(i,) for i in range(len(chains))]
    ends = [(None, sum((chains[i][1] for i in group), []), chains[group[0]][2]) for group in joined]
    alone = len(rep_bits) == 1
    states = [
        add(extra, [states[i][1] for i in group], [got[i] for i in group], alone)
        for group, (_, _, extra) in zip(joined, ends)
    ]
    for turn, (axis, bit) in enumerate(rep_bits[1:]):
        got = [swap(own, axis, bit) for own, _ in states]
        for i, (_, _, extra) in enumerate(ends):
            states[i] = add(extra, [states[i][0]], [got[i]], turn + 2 == len(rep_bits))
    others = [swap(bare, "rep", 1) for _, bare in states]
    outputs, grad_inputs = (home[:, i].reshape(inputs.shape) for i in range(2))
    factor = 1.0 / math.sqrt(reps * devs * rows)
    grad_e, grad_be, grad_r, grad_br, grad_gate = call(
        functools.partial(final_kernel, factor, ends),
        "final",
        [
            jax.ShapeDtypeStruct((both // devs, hid), F32),
            jax.ShapeDtypeStruct((1, hid), F32),
            jax.ShapeDtypeStruct((hid // devs, both), F32),
            jax.ShapeDtypeStruct((1, both), F32),
            jax.ShapeDtypeStruct((1, both), F32),
        ],
        (where, *[own for own, _ in states], *others),
        scalars=1,
    )
    return outputs, grad_inputs, grad_e, grad_be[0], grad_r, grad_br[0], grad_gate[0]


def solution(mesh):
    return jax.shard_map(
        body,
        mesh=mesh,
        in_specs=(P("rep", "ctx", None), P(), P(), P(), P(), P(), P("rep", "ctx", None)),
        out_specs=(
            P("rep", "ctx", None),
            P("rep", "ctx", None),
            P("ctx", None),
            P(),
            P("ctx", None),
            P(),
            P(),
        ),
        check_vma=False,
    )
```
